32 devices in a mesh: fsdp: 16 (over z, x, core), seq: 2 (over y).
Axes of the slice: x: 2, y: 2, z: 4, core: 2. Of those that a mesh axis runs over, the one named last changes fastest.
Arguments:
- tokens: bfloat16 [16, 1024, 768], P('fsdp', 'seq'), may hold values from -6 to 6
- cotangent: bfloat16 [16, 1024, 768], P('fsdp', 'seq'), may hold values from -6 to 6
- in_weight: float32 [768, 3352], P('fsdp'), may hold values from -0.21875 to 0.21875
- out_weight: float32 [1536, 768], P('fsdp'), may hold values from -0.15625 to 0.15625
- small_params: float32 [11336], replicated, as said below
- in_first: float32 [768, 3352], P('fsdp'), may hold values from -0.0008544922 to 0.0008544922
- in_second: float32 [768, 3352], P('fsdp'), may hold values from 2.6558167e-10 to 1.0623267e-09
- out_first: float32 [1536, 768], P('fsdp'), may hold values from -0.0008544922 to 0.0008544922
- out_second: float32 [1536, 768], P('fsdp'), may hold values from 2.6558167e-10 to 1.0623267e-09
- small_first: float32 [11336], replicated, may hold values from -0.0008544922 to 0.0008544922
- small_second: float32 [11336], replicated, may hold values from 2.6558167e-10 to 1.0623267e-09
Outputs:
- output: bfloat16 [16, 1024, 768], P('fsdp', 'seq')
- input_grad: float32 [16, 1024, 768], P('fsdp', 'seq')
- in_new: float32 [768, 3352], P('fsdp')
- in_first_new: float32 [768, 3352], P('fsdp')
- in_second_new: float32 [768, 3352], P('fsdp')
- out_new: float32 [1536, 768], P('fsdp')
- out_first_new: float32 [1536, 768], P('fsdp')
- out_second_new: float32 [1536, 768], P('fsdp')
- small_new: float32 [11336], replicated
- small_first_new: float32 [11336], replicated
- small_second_new: float32 [11336], replicated
- grad_norm: float32 [], replicated
The draws below stay inside these ranges and needn't reach their ends.
Inputs may be any that keep to these rules, and one draw needn't show every extreme that they name: `small_params`: gains near 1, convolution weights of deviation 0.5, convolution biases of deviation 0.2, time-step biases in -4 to -2, decay logarithms in -4.6 to -0.7, skip factors in 0.5 to 1.5, in the packed order.
All inputs are finite; a program needn't handle non-finite values.
Results may differ from the reference program's by a relative error of at most 0.02.
Values may be sent and summed in bfloat16 or wider, within the bound.
A program may use at most 80 MiB of HBM per device.

```python
import math
import jax
import jax.numpy as jnp
from jax import lax

D = 768
HEADS = 24
STATE = 128
HEAD_DIM = 64
CONV = 4
SPAN = 256
STEP = 10
INNER = 1536
CONV_CH = 1792
PROJ = 3352
SMALL = 11336
LENGTH = 1024
SEQS = 16


def draw_small_params(key, part):
    key = jax.random.fold_in(key, 11)
    keys = jax.random.split(key, 7)
    gain_in = 1.0 + 0.1 * jax.random.truncated_normal(keys[0], -3.0, 3.0, (D,), jnp.float32)
    gain_y = 1.0 + 0.1 * jax.random.truncated_normal(keys[1], -3.0, 3.0, (INNER,), jnp.float32)
    conv_w = 0.5 * jax.random.truncated_normal(keys[2], -3.0, 3.0, (CONV * CONV_CH,), jnp.float32)
    conv_b = 0.2 * jax.random.truncated_normal(keys[3], -3.0, 3.0, (CONV_CH,), jnp.float32)
    dt_bias = jax.random.uniform(keys[4], (HEADS,), jnp.float32, -4.0, -2.0)
    a_log = jax.random.uniform(keys[5], (HEADS,), jnp.float32, -4.6, -0.7)
    d_skip = jax.random.uniform(keys[6], (HEADS,), jnp.float32, 0.5, 1.5)
    return jnp.concatenate([gain_in, gain_y, conv_w, conv_b, dt_bias, a_log, d_skip]).astype(jnp.float32)


def level_of(stream_key, shape, pieces, least, high):
    factor_of, own = 1.0, jax.random.fold_in(stream_key, 6)
    for dim, blocks in pieces:
        heights = jnp.exp(jax.random.uniform(jax.random.fold_in(own, dim), (blocks,), jnp.float32, least / len(pieces), high / len(pieces)))
        factor_of = factor_of * jnp.repeat(heights, shape[dim] // blocks).reshape([-1 if axis == dim else 1 for axis in range(len(shape))])
    return factor_of


def normal_values(rng, shape, deviation, limit, pieces=(), kind=jnp.bfloat16):
    loudness = level_of(rng, shape, pieces, -0.22, 0.18) if pieces else 1.0
    values = jax.random.normal(rng, shape, jnp.float32) * deviation * loudness
    return jnp.minimum(jnp.maximum(values, -limit), limit).astype(kind)


def setup_inputs(seed: int = 0) -> dict:
    streams_of = jax.random.split(jax.random.key(seed), 12)
    return {
        "tokens": normal_values(streams_of[0], (SEQS, LENGTH, D), 1.0, 6.0, ((0, 16), (1, 2))),
        "cotangent": normal_values(streams_of[1], (SEQS, LENGTH, D), 1.0, 6.0, ((0, 16), (1, 2))),
        "in_weight": normal_values(streams_of[2], (D, PROJ), D ** -0.5, 0.21875, ((0, 16),), jnp.float32),
        "out_weight": normal_values(streams_of[3], (INNER, D), INNER ** -0.5, 0.15625, ((0, 16),), jnp.float32),
        "small_params": draw_small_params(jax.random.fold_in(streams_of[11], 71), 0),
        "in_first": normal_values(streams_of[5], (D, PROJ), (0.111 / (D * PROJ + INNER * D + SMALL) ** 0.5), 0.0008544922, ((0, 16),), jnp.float32),
        "in_second": jnp.clip(jnp.exp(math.log(1.0623266710751977e-09) - 1.3862944 * jax.random.uniform(streams_of[6], (D, PROJ), jnp.float32) ** level_of(streams_of[6], (D, PROJ), ((0, 16),), -0.2, 0.2)), 2.6558166776879943e-10, 1.0623266710751977e-09),
        "out_first": normal_values(streams_of[7], (INNER, D), (0.111 / (D * PROJ + INNER * D + SMALL) ** 0.5), 0.0008544922, ((0, 16),), jnp.float32),
        "out_second": jnp.clip(jnp.exp(math.log(1.0623266710751977e-09) - 1.3862944 * jax.random.uniform(streams_of[8], (INNER, D), jnp.float32) ** level_of(streams_of[8], (INNER, D), ((0, 16),), -0.2, 0.2)), 2.6558166776879943e-10, 1.0623266710751977e-09),
        "small_first": normal_values(streams_of[9], (SMALL,), (0.111 / (D * PROJ + INNER * D + SMALL) ** 0.5), 0.0008544922, (), jnp.float32),
        "small_second": jnp.clip(jnp.exp(jax.random.uniform(streams_of[10], (SMALL,), jnp.float32, math.log(2.6558166776879943e-10), math.log(1.0623266710751977e-09))), 2.6558166776879943e-10, 1.0623266710751977e-09),
    }


@jax.custom_vjp
def low(v):
    return lax.optimization_barrier(v.astype(jnp.bfloat16)).astype(jnp.float32)

@jax.custom_vjp
def low_back(v):
    return v

def low_keep(v):
    return (low(v), None)

def low_pass(kept, grad):
    return (grad,)

def back_keep(v):
    return (v, None)

def back_low(kept, grad):
    return (low(grad),)
low.defvjp(low_keep, low_pass)
low_back.defvjp(back_keep, back_low)
norm_eps = 1e-05
beta_one = 0.9
beta_two = 0.999
rate_big = 0.05
rate_small = 0.2
decay_big = 0.1
clip_level = 1.0
adam_eps = 1e-08
far_below = -1e+30
highest = lax.Precision.HIGHEST

def unpack(small_vec):
    first = D
    second = first + INNER
    third = second + CONV * CONV_CH
    fourth = third + CONV_CH
    fifth = fourth + HEADS
    sixth = fifth + HEADS
    return (small_vec[:first], small_vec[first:second], small_vec[second:third].reshape(CONV, CONV_CH), small_vec[third:fourth], small_vec[fourth:fifth], small_vec[fifth:sixth], small_vec[sixth:sixth + HEADS])

def rms_scale(values, gain):
    return values * lax.rsqrt(lax.optimization_barrier(jnp.mean(values * values, axis=-1, keepdims=True)) + norm_eps) * gain

def mix_in(padded, dt_raw, conv_w, conv_b, dt_bias):
    count = padded.shape[0] - (CONV - 1)
    summed = conv_b + conv_w[0] * padded[0:count]
    for offset in range(1, CONV):
        summed = summed + conv_w[offset] * padded[offset:offset + count]
    return (jax.nn.silu(summed), jax.nn.softplus(dt_raw + dt_bias))

def span_parts(head_vals, b_rows, c_rows, step_size, a_neg):
    count = head_vals.shape[0] // SPAN
    head_blk = head_vals.reshape(count, SPAN, HEADS, HEAD_DIM)
    b_blk = b_rows.reshape(count, SPAN, STATE)
    c_blk = c_rows.reshape(count, SPAN, STATE)
    step_blk = step_size.reshape(count, SPAN, HEADS).transpose(0, 2, 1)
    cum_log = jnp.cumsum(step_blk * a_neg[None, :, None], axis=2)
    lasts = cum_log[:, :, -1]
    inner = jnp.einsum('ctn,csn->cts', c_blk, b_blk, precision=highest)
    causal = lax.broadcasted_iota(jnp.int32, (SPAN, SPAN), 0) >= lax.broadcasted_iota(jnp.int32, (SPAN, SPAN), 1)
    spread = cum_log[:, :, :, None] - cum_log[:, :, None, :]
    mixing = jnp.exp(jnp.where(causal, spread, far_below)) * inner[:, None] * step_blk[:, :, None, :]
    diag_out = jnp.einsum('chts,cshp->cthp', mixing, head_blk, precision=highest)
    tail = jnp.exp(lasts[:, :, None] - cum_log) * step_blk
    states = jnp.einsum('chs,cshp,csn->chpn', tail, head_blk, b_blk, precision=highest)
    return (diag_out, states, lasts, cum_log, c_blk)

def chain(states, lasts, start):

    def advance(carry, item):
        block_state, block_last = item
        return (carry * jnp.exp(block_last)[:, None, None] + block_state, carry)
    return lax.scan(advance, start, (states, lasts))

def finish(diag_out, c_blk, cum_log, entering, head_vals, gate_vals, d_skip, gain_y):
    rows = diag_out.shape[0] * SPAN
    off_out = jnp.einsum('ctn,chpn->cthp', c_blk, entering, precision=highest) * jnp.exp(cum_log).transpose(0, 2, 1)[:, :, :, None]
    mixed = (diag_out + off_out).reshape(rows, INNER) + (head_vals * d_skip[None, :, None]).reshape(rows, INNER)
    gated = mixed * jax.nn.silu(gate_vals)
    return rms_scale(gated, gain_y)

def layer(inputs, in_weight, out_weight, small_vec):
    gain_in, gain_y, conv_w, conv_b, dt_bias, a_log, d_skip = unpack(small_vec)
    normed_in = rms_scale(inputs, gain_in)
    projected = low_back(low(jnp.dot(low(normed_in), low(in_weight), precision=highest)))
    gate_vals = projected[:, :INNER]
    conv_in = projected[:, INNER:INNER + CONV_CH]
    padded = jnp.concatenate([jnp.zeros_like(conv_in[:CONV - 1]), conv_in], axis=0)
    active, step_size = mix_in(padded, projected[:, INNER + CONV_CH:], conv_w, conv_b, dt_bias)
    head_vals = active[:, :INNER].reshape(-1, HEADS, HEAD_DIM)
    diag_out, states, lasts, cum_log, c_blk = span_parts(head_vals, active[:, INNER:INNER + STATE], active[:, INNER + STATE:], step_size, -jnp.exp(a_log))
    final_state, entering = chain(states, lasts, jnp.zeros_like(states[0]))
    normed_out = finish(diag_out, c_blk, cum_log, entering, head_vals, gate_vals, d_skip, gain_y)
    branch = low_back(jnp.dot(low(normed_out), low(out_weight), precision=highest))
    return inputs + branch

def adam_step(weight, grad, first, second, rate, decay):
    first_new = beta_one * first + (1.0 - beta_one) * grad
    second_new = beta_two * second + (1.0 - beta_two) * grad * grad
    first_hat = first_new / (1.0 - beta_one ** STEP)
    second_hat = second_new / (1.0 - beta_two ** STEP)
    weight_new = weight * (1.0 - rate * decay) - rate * first_hat / (jnp.sqrt(second_hat) + adam_eps)
    return (weight_new, first_new, second_new)

def reference(tokens, cotangent, in_weight, out_weight, small_params, in_first, in_second, out_first, out_second, small_first, small_second):

    def per_sequence(totals, item):
        inputs, upstream = item
        result, pullback = jax.vjp(layer, inputs.astype(jnp.float32), in_weight, out_weight, small_params)
        grad_inputs, grad_win, grad_wout, grad_small = pullback(upstream.astype(result.dtype))
        return ((totals[0] + grad_win, totals[1] + grad_wout, totals[2] + grad_small), (result.astype(jnp.bfloat16), grad_inputs))
    start = (jnp.zeros_like(in_weight), jnp.zeros_like(out_weight), jnp.zeros_like(small_params))
    totals, (output, input_grad) = lax.scan(per_sequence, start, (tokens, cotangent))
    grad_win, grad_wout, grad_small = totals
    grad_norm = jnp.sqrt(jnp.sum(grad_win * grad_win) + jnp.sum(grad_wout * grad_wout) + jnp.sum(grad_small * grad_small))
    factor = clip_level / jnp.maximum(grad_norm, clip_level)
    in_new, in_first_new, in_second_new = adam_step(in_weight, grad_win * factor, in_first, in_second, rate_big, decay_big)
    out_new, out_first_new, out_second_new = adam_step(out_weight, grad_wout * factor, out_first, out_second, rate_big, decay_big)
    small_new, small_first_new, small_second_new = adam_step(small_params, grad_small * factor, small_first, small_second, rate_small, 0.0)
    return (output, input_grad, in_new, in_first_new, in_second_new, out_new, out_first_new, out_second_new, small_new, small_first_new, small_second_new, grad_norm)
```

```python
import jax
import jax.numpy as jnp
from jax import lax
from jax.experimental import pallas as pl
from jax.experimental.pallas import tpu as pltpu
import functools
from jax.sharding import PartitionSpec as P

D = 768
HEADS = 24
STATE = 128
HEAD_DIM = 64
CONV = 4
SPAN = 256
STEP = 10
INNER = 1536
CONV_CH = 1792
PROJ = 3352


norm_eps = 1e-05
beta_one = 0.9
beta_two = 0.999
rate_big = 0.05
rate_small = 0.2
decay_big = 0.1
clip_level = 1.0
adam_eps = 1e-08
far_below = -1e30
highest = lax.Precision.HIGHEST


UR = PROJ - INNER
LANES = 128
PAIRS = INNER // LANES
SMALL = D + INNER + (CONV + 1) * CONV_CH + 3 * HEADS
vmem_bytes = 58 * 1024 * 1024


def rms_scale(values, gain):
    return values * lax.rsqrt(jnp.mean(values * values, axis=-1, keepdims=True) + norm_eps) * gain


def dot(a, b):
    return jnp.dot(a, b, preferred_element_type=jnp.float32)


def dot_rows(a, b):
    return lax.dot_general(a, b, (((1,), (1,)), ((), ())), preferred_element_type=jnp.float32)


def dot_full(a, b):
    return jnp.dot(a, b, precision=highest, preferred_element_type=jnp.float32)


def low(a):
    return a.astype(jnp.bfloat16)


def grid_of(shape, dim):
    return lax.broadcasted_iota(jnp.int32, shape, dim)


def expander():
    shape = (LANES, INNER)
    return (grid_of(shape, 1) // HEAD_DIM == grid_of(shape, 0)).astype(jnp.float32)


def pair_sum(pair):
    shape = (LANES, LANES)
    return (grid_of(shape, 0) // HEAD_DIM + 2 * pair == grid_of(shape, 1)).astype(jnp.float32)


def paired(values, pair):
    rows = values.shape[0]
    left = jnp.broadcast_to(values[:, 2 * pair : 2 * pair + 1], (rows, LANES))
    right = jnp.broadcast_to(values[:, 2 * pair + 1 : 2 * pair + 2], (rows, LANES))
    return jnp.where(grid_of((rows, LANES), 1) < HEAD_DIM, left, right)


def conv_at(upad, conv_w, conv_b, count, columns):
    summed = conv_b[:, columns] + conv_w[0:1, columns] * upad[5 : 5 + count, columns]
    for k in range(1, CONV):
        summed = summed + conv_w[k : k + 1, columns] * upad[5 + k : 5 + k + count, columns]
    return summed


def softplus(x):
    return jnp.maximum(x, 0.0) + jnp.log1p(jnp.exp(-jnp.abs(x)))


def span_rows(c):
    return pl.ds(pl.multiple_of(c * SPAN, SPAN), SPAN)


def scan_kernel(ur, rim, conv_w, conv_b, dtb, a_neg, act, step, cum_out, yraw, entering, state, upad):
    count = ur.shape[0]
    blocks = count // SPAN
    upad[0:8] = rim[...].astype(jnp.float32)
    upad[8 : 8 + count] = ur[:, :CONV_CH].astype(jnp.float32)
    for first in range(0, CONV_CH, 256):
        columns = slice(first, first + 256)
        summed = conv_at(upad, conv_w, conv_b, count, columns)
        act[:, columns] = summed * jax.nn.sigmoid(summed)
    step[...] = jnp.zeros_like(step)
    step[:, :HEADS] = softplus(ur[:, CONV_CH:].astype(jnp.float32) + dtb[:, :HEADS])
    state[...] = jnp.zeros_like(state)
    at, along = (grid_of((SPAN, SPAN), 0), grid_of((SPAN, SPAN), 1))
    causal = at >= along
    tril = causal.astype(jnp.float32)
    left = grid_of((SPAN, LANES), 1) < HEAD_DIM

    def span(c, carry):
        rows = span_rows(c)
        entering[pl.ds(c, 1)] = state[...][None]
        dt = step[rows, :]
        cum = dot_full(tril, dt * a_neg[...])
        cum_out[rows, :] = cum
        cum_t = cum.T
        last = cum[SPAN - 1 : SPAN, :]
        grow, tail, whole = (jnp.exp(cum), jnp.exp(last - cum) * dt, jnp.exp(last))
        b_vals = act[rows, INNER : INNER + STATE]
        b_t = low(b_vals.T)
        c_low = low(act[rows, INNER + STATE :])
        inner = dot_rows(c_low, low(b_vals))
        for pair in range(PAIRS):
            lanes = slice(pair * LANES, (pair + 1) * LANES)
            v = act[rows, lanes]
            x_low = low(v * paired(dt, pair))
            sides = []
            for h in (2 * pair, 2 * pair + 1):
                spread = jnp.where(causal, cum[:, h : h + 1] - cum_t[h : h + 1, :], far_below)
                sides.append(dot(low(jnp.exp(spread) * inner), x_low))
            was = state[:, lanes]
            yraw[rows, lanes] = jnp.where(left, sides[0], sides[1]) + paired(grow, pair) * dot(
                c_low, low(was)
            )
            state[:, lanes] = was * paired(whole, pair) + dot(b_t, low(v * paired(tail, pair)))
        return carry

    lax.fori_loop(0, blocks, span, 0)


def gate_kernel(yraw, act, cum_ref, start, z_ref, up, gain, skip, ymix, out, dz, dy, sums, dstart, held, run):
    count = yraw.shape[0]
    blocks = count // SPAN
    expand = expander()
    held[...] = start[...].astype(jnp.float32)
    run[...] = jnp.ones_like(run)
    sums[...] = jnp.zeros_like(sums)
    dstart[...] = jnp.zeros_like(dstart)

    def span(c, carry):
        rows = span_rows(c)
        cum = cum_ref[rows, :]
        grow = dot_full(jnp.exp(cum), expand)
        c_vals = act[rows, INNER + STATE : CONV_CH]
        raw = yraw[rows, :] + grow * dot(low(c_vals), low(held[...]))
        ymix[rows, :] = raw
        v = act[rows, :INNER]
        scanned = raw + skip[...] * v
        z = z_ref[rows, :].astype(jnp.float32)
        sig = jax.nn.sigmoid(z)
        gated = scanned * (z * sig)
        scale = lax.rsqrt(jnp.mean(gated * gated, axis=1, keepdims=True) + norm_eps)
        unit = gated * scale
        out[rows, :] = low(unit * gain[...])
        grad = up[rows, :]
        sums[0:1] += jnp.sum(grad * unit, axis=0, keepdims=True)
        grad = grad * gain[...]
        grad = scale * (grad - unit * jnp.mean(grad * unit, axis=1, keepdims=True))
        dz[rows, :] = low(grad * scanned * (sig * (1.0 + z * (1.0 - sig))))
        grad = grad * (z * sig)
        dy[rows, :] = grad
        sums[1:2] += jnp.sum(grad * v, axis=0, keepdims=True)
        dstart[...] += run[0:1] * dot(low(c_vals.T), low(grow * grad))
        whole = grow[SPAN - 1 : SPAN, :]
        held[...] = held[...] * whole
        run[...] = run[...] * whole
        return carry

    lax.fori_loop(0, blocks, span, 0)


def back_kernel(
    ur, rim, conv_w, conv_b, dtb, a_neg, act, step, cum_ref, ymix, entering, start, later, dy_ref, skip,
    gp, du_tail, du_rim, dconv_w, dheads, upad, dcp, dact, leave, before, dinner,
):
    count = ur.shape[0]
    blocks = count // SPAN
    dheads[...] = jnp.zeros_like(dheads)
    leave[...] = later[...].astype(jnp.float32)
    at, along = (grid_of((SPAN, SPAN), 0), grid_of((SPAN, SPAN), 1))
    causal = at <= along
    triu = causal.astype(jnp.float32)
    left = grid_of((SPAN, LANES), 1) < HEAD_DIM
    expand = expander()
    before[0] = start[...].astype(jnp.float32)
    for c in range(1, blocks):
        ends = jnp.exp(jnp.broadcast_to(cum_ref[c * SPAN - 1 : c * SPAN, :], (8, LANES)))
        before[c] = before[c - 1] * dot_full(ends, expand)[0:1]

    def span(lap, carry):
        c = blocks - 1 - lap
        rows = span_rows(c)
        dt, cum = (step[rows, :], cum_ref[rows, :])
        cum_t = cum.T
        last = cum[SPAN - 1 : SPAN, :]
        grow, fade, whole = (jnp.exp(cum), jnp.exp(last - cum), jnp.exp(last))
        b_vals, c_vals = (act[rows, INNER : INNER + STATE], act[rows, INNER + STATE : CONV_CH])
        b_low, c_low, c_t = (low(b_vals), low(c_vals), low(c_vals.T))
        inner = dot_rows(b_low, c_low)
        db = jnp.zeros((SPAN, STATE), jnp.float32)
        dc = jnp.zeros((SPAN, STATE), jnp.float32)
        dt_part = jnp.zeros((SPAN, LANES), jnp.float32)
        out_part = jnp.zeros((SPAN, LANES), jnp.float32)
        end_part = jnp.zeros((8, LANES), jnp.float32)
        dinner[...] = jnp.zeros_like(dinner)
        for pair in range(PAIRS):
            lanes = slice(pair * LANES, (pair + 1) * LANES)
            pick = pair_sum(pair)
            v, dy = (act[rows, lanes], dy_ref[rows, lanes])
            dtp, fadep, wholep = (paired(dt, pair), paired(fade, pair), paired(whole, pair))
            x = v * dtp
            dy_low = low(dy)
            sides = []
            for h, mine in ((2 * pair, left), (2 * pair + 1, ~left)):
                decay = jnp.exp(
                    jnp.where(causal, cum_t[h : h + 1, :] - cum[:, h : h + 1], far_below)
                )
                sides.append(dot(low(decay * inner), dy_low))
                dinner[...] += decay * dot_rows(low(jnp.where(mine, x, 0.0)), dy_low)
            g = leave[:, lanes]
            g_low = low(g)
            e = entering[pl.ds(c, 1), :, lanes][0] + before[pl.ds(c, 1), :, lanes][0]
            from_state = fadep * dot(b_low, g_low)
            dx = jnp.where(left, sides[0], sides[1]) + from_state
            dact[rows, lanes] = dtp * dx + skip[:, lanes] * dy
            grown = low(paired(grow, pair) * dy)
            dc = dc + dot_rows(grown, low(e))
            db = db + dot_rows(low(x * fadep), g_low)
            dt_part = dt_part + dot_full(v * dx, pick)
            out_part = out_part + dot_full(dy * ymix[rows, lanes], pick)
            ends = wholep * jnp.sum(e * g, axis=0, keepdims=True) + jnp.sum(
                x * from_state, axis=0, keepdims=True
            )
            end_part = end_part + dot_full(jnp.broadcast_to(ends, (8, LANES)), pick)
            leave[:, lanes] = g * wholep + dot(c_t, grown)
        d_in = dinner[...]
        dact[rows, INNER : INNER + STATE] = db + dot(low(d_in), c_low)
        dact[rows, INNER + STATE : CONV_CH] = dc + dot(low(d_in.T), b_low)
        dcum = out_part - dt * dt_part
        dcum = dcum + jnp.where(grid_of((SPAN, LANES), 0) == SPAN - 1, end_part[0:1], 0.0)
        rate = dot_full(triu, dcum)
        raw = ur[rows, CONV_CH:].astype(jnp.float32) + dtb[:, :HEADS]
        dr = (dt_part + a_neg[...] * rate)[:, :HEADS] * jax.nn.sigmoid(raw)
        gp[rows, CONV_CH:] = low(dr)
        dheads[0:1, :HEADS] += jnp.sum(dr, axis=0, keepdims=True)
        dheads[1:2] += jnp.sum(dt * rate, axis=0, keepdims=True) * a_neg[...]
        return carry

    lax.fori_loop(0, blocks, span, 0)
    upad[0:8] = rim[...].astype(jnp.float32)
    upad[8 : 8 + count] = ur[:, :CONV_CH].astype(jnp.float32)
    dcp[0:8] = jnp.zeros((8, CONV_CH), jnp.float32)
    dcp[8 + count : 16 + count] = jnp.zeros((8, CONV_CH), jnp.float32)
    dconv_w[...] = jnp.zeros_like(dconv_w)
    for first in range(0, CONV_CH, 256):
        columns = slice(first, first + 256)
        summed = conv_at(upad, conv_w, conv_b, count, columns)
        sig = jax.nn.sigmoid(summed)
        dconv = dact[:, columns] * (sig * (1.0 + summed * (1.0 - sig)))
        dcp[8 : 8 + count, columns] = dconv
        for k in range(CONV):
            dconv_w[k : k + 1, columns] = jnp.sum(
                dconv * upad[5 + k : 5 + k + count, columns], axis=0, keepdims=True
            )
        dconv_w[CONV : CONV + 1, columns] = jnp.sum(dconv, axis=0, keepdims=True)
        du = conv_w[0:1, columns] * dcp[3 : 3 + count + 8, columns]
        for k in range(1, CONV):
            du = du + conv_w[k : k + 1, columns] * dcp[3 - k : 3 - k + count + 8, columns]
        du_rim[:, columns] = du[0:8]
        du_tail[:, columns] = du[count : count + 8]
        gp[:, columns] = low(du[8:])


def local_call(kernel, outs, scratch, flops):
    return pl.pallas_call(
        kernel,
        out_shape=[jax.ShapeDtypeStruct(shape, kind) for shape, kind in outs],
        out_specs=[pl.BlockSpec(memory_space=pltpu.VMEM)] * len(outs),
        scratch_shapes=[pltpu.VMEM(shape, jnp.float32) for shape in scratch],
        compiler_params=pltpu.CompilerParams(vmem_limit_bytes=vmem_bytes),
        cost_estimate=pl.CostEstimate(flops=flops, bytes_accessed=20_000_000, transcendentals=0),
    )


def total_kernel(n, vec, square, total, squares, land, mine, sq_land, sq_mine, s1, r1, s2, r2, s3, r3):
    me = lax.axis_index("fsdp")
    rows = land.shape[1]
    barrier = pltpu.get_barrier_semaphore()

    def peer(k):
        return lax.rem(me + k, n)

    def greet(k, carry):
        pl.semaphore_signal(
            barrier, inc=1, device_id={"fsdp": peer(k)}, device_id_type=pl.DeviceIdType.MESH
        )
        return carry

    lax.fori_loop(1, n, greet, 0)
    pl.semaphore_wait(barrier, n - 1)

    def remote(k, src, dst, send, recv):
        return pltpu.make_async_remote_copy(
            src_ref=src,
            dst_ref=dst,
            send_sem=send.at[k],
            recv_sem=recv.at[k],
            device_id={"fsdp": peer(k)},
            device_id_type=pl.DeviceIdType.MESH,
        )

    def share(k):
        chunk = pl.ds(pl.multiple_of(peer(k) * rows, 8), rows)
        return remote(k, vec.at[chunk], land.at[k], s1, r1)

    def part(k):
        return remote(k, square, sq_land.at[k], s3, r3)

    def whole(k):
        chunk = pl.ds(pl.multiple_of(me * rows, 8), rows)
        return remote(k, mine, total.at[chunk], s2, r2)

    def each(act):
        def step(k, carry):
            act(k)
            return carry

        lax.fori_loop(1, n, step, 0)

    def begin(k):
        share(k).start()
        part(k).start()

    each(begin)
    own = pl.ds(pl.multiple_of(me * rows, 8), rows)
    each(lambda k: share(k).wait())
    summed = vec[own, :]
    for k in range(1, n):
        summed = summed + land[k]
    mine[...] = summed
    total[own, :] = summed
    each(lambda k: whole(k).start())
    each(lambda k: part(k).wait())
    gathered = square[...]
    for k in range(1, n):
        gathered = gathered + sq_land[k]
    squares[...] = gathered
    each(lambda k: whole(k).wait())


def total_call(n, vec, square):
    rows = vec.shape[0] // n
    dma = pltpu.SemaphoreType.DMA((n,))
    return pl.pallas_call(
        functools.partial(total_kernel, n),
        out_shape=[
            jax.ShapeDtypeStruct(vec.shape, jnp.float32),
            jax.ShapeDtypeStruct(square.shape, jnp.float32),
        ],
        in_specs=[pl.BlockSpec(memory_space=pltpu.VMEM)] * 2,
        out_specs=[pl.BlockSpec(memory_space=pltpu.VMEM)] * 2,
        scratch_shapes=[
            pltpu.VMEM((n, rows, LANES), jnp.float32),
            pltpu.VMEM((rows, LANES), jnp.float32),
            pltpu.VMEM((n, 8, LANES), jnp.float32),
            pltpu.VMEM((8, LANES), jnp.float32),
        ]
        + [dma] * 6,
        compiler_params=pltpu.CompilerParams(collective_id=0, has_side_effects=True),
    )(vec, square)


def adam_step(weight, grad, first, second, rate, decay):
    first_new = beta_one * first + (1.0 - beta_one) * grad
    second_new = beta_two * second + (1.0 - beta_two) * grad * grad
    first_hat = first_new / (1.0 - beta_one**STEP)
    second_hat = second_new / (1.0 - beta_two**STEP)
    weight_new = weight * (1.0 - rate * decay) - rate * first_hat / (
        jnp.sqrt(second_hat) + adam_eps
    )
    return (weight_new, first_new, second_new)


def passed_along(value, axis, steps):
    count = lax.axis_size(axis)
    first, last = (max(0, -steps), min(count, count - steps))
    return lax.ppermute(value, axis, [(source, source + steps) for source in range(first, last)])


def carried(value, decay, axis, steps):
    arrived = passed_along(low(value), axis, steps)
    for _ in range(lax.axis_size(axis) - 2):
        arrived = passed_along(low(value + decay * arrived.astype(jnp.float32)), axis, steps)
    return arrived


def summed_over(value, axis):
    if lax.axis_size(axis) == 2:
        return value.astype(jnp.float32) + lax.ppermute(value, axis, [(0, 1), (1, 0)]).astype(
            jnp.float32
        )
    return lax.psum(value.astype(jnp.float32), axis)


def head_lanes(values):
    return jnp.repeat(values, HEAD_DIM)[None]


def shards(
    tokens,
    cotangent,
    in_weight,
    out_weight,
    small_params,
    in_first,
    in_second,
    out_first,
    out_second,
    small_first,
    small_second,
):
    inputs = tokens[0].astype(jnp.float32)
    upstream_low = cotangent[0]
    upstream = upstream_low.astype(jnp.float32)
    count = inputs.shape[0]
    blocks = count // SPAN
    fsdp = lax.axis_size("fsdp")
    f32, bf16 = (jnp.float32, jnp.bfloat16)

    def gathered(shard):
        return lax.all_gather(low(shard), "fsdp", axis=0, tiled=True)

    win_ur = gathered(in_weight[:, INNER:])
    win_z = gathered(in_weight[:, :INNER])
    wout = gathered(out_weight)

    cuts = [D, D + INNER, D + INNER + CONV * CONV_CH, D + INNER + (CONV + 1) * CONV_CH]
    gain_in = small_params[: cuts[0]]
    gain_y = small_params[cuts[0] : cuts[1]][None]
    conv_w = small_params[cuts[1] : cuts[2]].reshape(CONV, CONV_CH)
    conv_b = small_params[cuts[2] : cuts[3]][None]
    dt_bias, a_log, d_skip = small_params[cuts[3] :].reshape(3, HEADS)
    dtb = jnp.pad(dt_bias, (0, LANES - HEADS))[None]
    a_neg = jnp.pad(-jnp.exp(a_log), (0, LANES - HEADS))[None]
    skip = head_lanes(d_skip)

    normed_in, pull_norm = jax.vjp(rms_scale, inputs, gain_in)
    normed_low = low(normed_in)
    ur = dot(normed_low, win_ur).astype(bf16)
    rim = passed_along(ur[count - 8 :, :CONV_CH], "seq", 1)
    wide, heads = ((count, INNER), (count, LANES))
    act, step, cum, yraw, entering, dev_state = local_call(
        scan_kernel,
        [
            ((count, CONV_CH), f32),
            (heads, f32),
            (heads, f32),
            (wide, f32),
            ((blocks, STATE, INNER), f32),
            ((STATE, INNER), f32),
        ],
        [(count + 8, CONV_CH)],
        8_000_000_000,
    )(ur, rim, conv_w, conv_b, dtb, a_neg)
    dev_decay = head_lanes(jnp.exp(jnp.sum(cum[SPAN - 1 :: SPAN, :HEADS], axis=0)))
    start = carried(dev_state, dev_decay, "seq", 1)
    z = dot(normed_low, win_z).astype(bf16)
    grad_normed = dot_rows(upstream_low, wout)
    ymix, out_low, dz, dy, gate_sums, dstart = local_call(
        gate_kernel,
        [
            (wide, f32),
            (wide, bf16),
            (wide, bf16),
            (wide, f32),
            ((8, INNER), f32),
            ((STATE, INNER), f32),
        ],
        [(STATE, INNER), (8, INNER)],
        8_000_000_000,
    )(yraw, act, cum, start, z, grad_normed, gain_y, skip)
    later = carried(dstart, dev_decay, "seq", -1)

    def shared(grad):
        return lax.psum_scatter(low(grad), "fsdp", scatter_dimension=0, tiled=True)

    own_z = shared(dot(normed_low.T, dz))
    own_wout = shared(dot(out_low.T, upstream_low))
    output = low(inputs + dot(out_low, wout))[None]
    gp, du_tail, du_rim, dconv, dheads = local_call(
        back_kernel,
        [
            ((count, UR), bf16),
            ((8, CONV_CH), f32),
            ((8, CONV_CH), f32),
            ((8, CONV_CH), f32),
            ((8, LANES), f32),
        ],
        [
            (count + 8, CONV_CH),
            (count + 16, CONV_CH),
            (count, CONV_CH),
            (STATE, INNER),
            (blocks, STATE, INNER),
            (SPAN, SPAN),
        ],
        20_000_000_000,
    )(ur, rim, conv_w, conv_b, dtb, a_neg, act, step, cum, ymix, entering, start, later, dy, skip)
    rim_return = passed_along(du_rim, "seq", -1)
    gp = lax.dynamic_update_slice(gp, low(du_tail + rim_return), (count - 8, 0))
    own_ur = shared(dot(normed_low.T, gp))
    grad_normed_in = dot_rows(dz, win_z) + dot_rows(gp, win_ur)
    grad_inputs, grad_gain = pull_norm(grad_normed_in)
    input_grad = (upstream + grad_inputs)[None]
    grad_small = jnp.concatenate(
        [
            grad_gain,
            gate_sums[0],
            dconv[: CONV + 1].reshape(-1),
            dheads[0, :HEADS],
            dheads[1, :HEADS],
            jnp.sum(gate_sums[1].reshape(HEADS, HEAD_DIM), axis=1),
        ]
    )
    chunk = -(-SMALL // (fsdp * 8 * LANES)) * 8 * LANES
    grad_small = jnp.pad(grad_small, (0, chunk * fsdp - SMALL)).reshape(-1, LANES)
    grad_small = summed_over(grad_small, "seq")
    own_z = summed_over(own_z, "seq")
    own_wout = summed_over(own_wout, "seq")
    own_ur = summed_over(own_ur, "seq")
    local_square = jnp.sum(own_z * own_z) + jnp.sum(own_wout * own_wout) + jnp.sum(own_ur * own_ur)
    grad_small, squares = total_call(fsdp, grad_small, jnp.full((8, LANES), local_square, f32))
    grad_small = grad_small.reshape(-1)[:SMALL]
    grad_norm = jnp.sqrt(squares[0, 0] + jnp.sum(grad_small * grad_small))
    factor = clip_level / jnp.maximum(grad_norm, clip_level)
    own_win = jnp.concatenate([own_z, own_ur], axis=1)
    in_new, in_first_new, in_second_new = adam_step(
        in_weight, own_win * factor, in_first, in_second, rate_big, decay_big
    )
    out_new, out_first_new, out_second_new = adam_step(
        out_weight, own_wout * factor, out_first, out_second, rate_big, decay_big
    )
    small_new, small_first_new, small_second_new = adam_step(
        small_params, grad_small * factor, small_first, small_second, rate_small, 0.0
    )
    return (
        output,
        input_grad,
        in_new,
        in_first_new,
        in_second_new,
        out_new,
        out_first_new,
        out_second_new,
        small_new,
        small_first_new,
        small_second_new,
        grad_norm,
    )


def solution(mesh):
    return jax.shard_map(
        shards,
        mesh=mesh,
        in_specs=(
            P("fsdp", "seq", None),
            P("fsdp", "seq", None),
            P("fsdp", None),
            P("fsdp", None),
            P(),
            P("fsdp", None),
            P("fsdp", None),
            P("fsdp", None),
            P("fsdp", None),
            P(),
            P(),
        ),
        out_specs=(
            P("fsdp", "seq", None),
            P("fsdp", "seq", None),
            P("fsdp", None),
            P("fsdp", None),
            P("fsdp", None),
            P("fsdp", None),
            P("fsdp", None),
            P("fsdp", None),
            P(),
            P(),
            P(),
            P(),
        ),
        check_vma=False,
    )
```

```python
import jax
import jax.numpy as jnp
from jax import lax
from jax.experimental import pallas as pl
from jax.experimental.pallas import tpu as pltpu
import functools
from jax.sharding import PartitionSpec as P

D = 768
HEADS = 24
STATE = 128
HEAD_DIM = 64
CONV = 4
SPAN = 256
STEP = 10
INNER = 1536
CONV_CH = 1792
PROJ = 3352


norm_eps = 1e-05
beta_one = 0.9
beta_two = 0.999
rate_big = 0.05
rate_small = 0.2
decay_big = 0.1
clip_level = 1.0
adam_eps = 1e-08
far_below = -1e30
highest = lax.Precision.HIGHEST


UR = PROJ - INNER
LANES = 128
PAIRS = INNER // LANES
SMALL = D + INNER + (CONV + 1) * CONV_CH + 3 * HEADS
vmem_bytes = 58 * 1024 * 1024


def rms_scale(values, gain):
    return values * lax.rsqrt(jnp.mean(values * values, axis=-1, keepdims=True) + norm_eps) * gain


def dot(a, b):
    return jnp.dot(a, b, preferred_element_type=jnp.float32)


def dot_rows(a, b):
    return lax.dot_general(a, b, (((1,), (1,)), ((), ())), preferred_element_type=jnp.float32)


def dot_full(a, b):
    return jnp.dot(a, b, precision=highest, preferred_element_type=jnp.float32)


def low(a):
    return a.astype(jnp.bfloat16)


def grid_of(shape, dim):
    return lax.broadcasted_iota(jnp.int32, shape, dim)


def expander():
    shape = (LANES, INNER)
    return (grid_of(shape, 1) // HEAD_DIM == grid_of(shape, 0)).astype(jnp.float32)


def pair_sum(pair):
    shape = (LANES, LANES)
    return (grid_of(shape, 0) // HEAD_DIM + 2 * pair == grid_of(shape, 1)).astype(jnp.float32)


def paired(values, pair):
    rows = values.shape[0]
    left = jnp.broadcast_to(values[:, 2 * pair : 2 * pair + 1], (rows, LANES))
    right = jnp.broadcast_to(values[:, 2 * pair + 1 : 2 * pair + 2], (rows, LANES))
    return jnp.where(grid_of((rows, LANES), 1) < HEAD_DIM, left, right)


def conv_at(upad, conv_w, conv_b, count, columns):
    summed = conv_b[:, columns] + conv_w[0:1, columns] * upad[5 : 5 + count, columns]
    for k in range(1, CONV):
        summed = summed + conv_w[k : k + 1, columns] * upad[5 + k : 5 + k + count, columns]
    return summed


def softplus(x):
    return jnp.maximum(x, 0.0) + jnp.log1p(jnp.exp(-jnp.abs(x)))


def span_rows(c):
    return pl.ds(pl.multiple_of(c * SPAN, SPAN), SPAN)


def scan_kernel(ur, rim, conv_w, conv_b, dtb, a_neg, act, step, cum_out, yraw, entering, state, upad):
    count = ur.shape[0]
    blocks = count // SPAN
    upad[0:8] = rim[...].astype(jnp.float32)
    upad[8 : 8 + count] = ur[:, :CONV_CH].astype(jnp.float32)
    for first in range(0, CONV_CH, 256):
        columns = slice(first, first + 256)
        summed = conv_at(upad, conv_w, conv_b, count, columns)
        act[:, columns] = summed * jax.nn.sigmoid(summed)
    step[...] = jnp.zeros_like(step)
    step[:, :HEADS] = softplus(ur[:, CONV_CH:].astype(jnp.float32) + dtb[:, :HEADS])
    state[...] = jnp.zeros_like(state)
    at, along = (grid_of((SPAN, SPAN), 0), grid_of((SPAN, SPAN), 1))
    causal = at >= along
    tril = causal.astype(jnp.float32)
    left = grid_of((SPAN, LANES), 1) < HEAD_DIM

    def span(c, carry):
        rows = span_rows(c)
        entering[pl.ds(c, 1)] = state[...][None]
        dt = step[rows, :]
        cum = dot_full(tril, dt * a_neg[...])
        cum_out[rows, :] = cum
        cum_t = cum.T
        last = cum[SPAN - 1 : SPAN, :]
        grow, tail, whole = (jnp.exp(cum), jnp.exp(last - cum) * dt, jnp.exp(last))
        b_vals = act[rows, INNER : INNER + STATE]
        b_t = low(b_vals.T)
        c_low = low(act[rows, INNER + STATE :])
        inner = dot_rows(c_low, low(b_vals))
        for pair in range(PAIRS):
            lanes = slice(pair * LANES, (pair + 1) * LANES)
            v = act[rows, lanes]
            x_low = low(v * paired(dt, pair))
            sides = []
            for h in (2 * pair, 2 * pair + 1):
                spread = jnp.where(causal, cum[:, h : h + 1] - cum_t[h : h + 1, :], far_below)
                sides.append(dot(low(jnp.exp(spread) * inner), x_low))
            was = state[:, lanes]
            yraw[rows, lanes] = jnp.where(left, sides[0], sides[1]) + paired(grow, pair) * dot(
                c_low, low(was)
            )
            state[:, lanes] = was * paired(whole, pair) + dot(b_t, low(v * paired(tail, pair)))
        return carry

    lax.fori_loop(0, blocks, span, 0)


def gate_kernel(yraw, act, cum_ref, start, z_ref, up, gain, skip, ymix, out, dz, dy, sums, dstart, held, run):
    count = yraw.shape[0]
    blocks = count // SPAN
    expand = expander()
    held[...] = start[...].astype(jnp.float32)
    run[...] = jnp.ones_like(run)
    sums[...] = jnp.zeros_like(sums)
    dstart[...] = jnp.zeros_like(dstart)

    def span(c, carry):
        rows = span_rows(c)
        cum = cum_ref[rows, :]
        grow = dot_full(jnp.exp(cum), expand)
        c_vals = act[rows, INNER + STATE : CONV_CH]
        raw = yraw[rows, :] + grow * dot(low(c_vals), low(held[...]))
        ymix[rows, :] = raw
        v = act[rows, :INNER]
        scanned = raw + skip[...] * v
        z = z_ref[rows, :].astype(jnp.float32)
        sig = jax.nn.sigmoid(z)
        gated = scanned * (z * sig)
        scale = lax.rsqrt(jnp.mean(gated * gated, axis=1, keepdims=True) + norm_eps)
        unit = gated * scale
        out[rows, :] = low(unit * gain[...])
        grad = up[rows, :]
        sums[0:1] += jnp.sum(grad * unit, axis=0, keepdims=True)
        grad = grad * gain[...]
        grad = scale * (grad - unit * jnp.mean(grad * unit, axis=1, keepdims=True))
        dz[rows, :] = low(grad * scanned * (sig * (1.0 + z * (1.0 - sig))))
        grad = grad * (z * sig)
        dy[rows, :] = grad
        sums[1:2] += jnp.sum(grad * v, axis=0, keepdims=True)
        dstart[...] += run[0:1] * dot(low(c_vals.T), low(grow * grad))
        whole = grow[SPAN - 1 : SPAN, :]
        held[...] = held[...] * whole
        run[...] = run[...] * whole
        return carry

    lax.fori_loop(0, blocks, span, 0)


def back_kernel(
    ur, rim, conv_w, conv_b, dtb, a_neg, act, step, cum_ref, ymix, entering, start, later, dy_ref, skip,
    gp, du_tail, du_rim, dconv_w, dheads, upad, dcp, dact, leave, before, dinner,
):
    count = ur.shape[0]
    blocks = count // SPAN
    dheads[...] = jnp.zeros_like(dheads)
    leave[...] = later[...].astype(jnp.float32)
    at, along = (grid_of((SPAN, SPAN), 0), grid_of((SPAN, SPAN), 1))
    causal = at <= along
    triu = causal.astype(jnp.float32)
    left = grid_of((SPAN, LANES), 1) < HEAD_DIM
    expand = expander()
    before[0] = start[...].astype(jnp.float32)
    for c in range(1, blocks):
        ends = jnp.exp(jnp.broadcast_to(cum_ref[c * SPAN - 1 : c * SPAN, :], (8, LANES)))
        before[c] = before[c - 1] * dot_full(ends, expand)[0:1]

    def span(lap, carry):
        c = blocks - 1 - lap
        rows = span_rows(c)
        dt, cum = (step[rows, :], cum_ref[rows, :])
        cum_t = cum.T
        last = cum[SPAN - 1 : SPAN, :]
        grow, fade, whole = (jnp.exp(cum), jnp.exp(last - cum), jnp.exp(last))
        b_vals, c_vals = (act[rows, INNER : INNER + STATE], act[rows, INNER + STATE : CONV_CH])
        b_low, c_low, c_t = (low(b_vals), low(c_vals), low(c_vals.T))
        inner = dot_rows(b_low, c_low)
        db = jnp.zeros((SPAN, STATE), jnp.float32)
        dc = jnp.zeros((SPAN, STATE), jnp.float32)
        dt_part = jnp.zeros((SPAN, LANES), jnp.float32)
        out_part = jnp.zeros((SPAN, LANES), jnp.float32)
        end_part = jnp.zeros((8, LANES), jnp.float32)
        dinner[...] = jnp.zeros_like(dinner)
        for pair in range(PAIRS):
            lanes = slice(pair * LANES, (pair + 1) * LANES)
            pick = pair_sum(pair)
            v, dy = (act[rows, lanes], dy_ref[rows, lanes])
            dtp, fadep, wholep = (paired(dt, pair), paired(fade, pair), paired(whole, pair))
            x = v * dtp
            dy_low = low(dy)
            sides = []
            for h, mine in ((2 * pair, left), (2 * pair + 1, ~left)):
                decay = jnp.exp(
                    jnp.where(causal, cum_t[h : h + 1, :] - cum[:, h : h + 1], far_below)
                )
                sides.append(dot(low(decay * inner), dy_low))
                dinner[...] += decay * dot_rows(low(jnp.where(mine, x, 0.0)), dy_low)
            g = leave[:, lanes]
            g_low = low(g)
            e = entering[pl.ds(c, 1), :, lanes][0] + before[pl.ds(c, 1), :, lanes][0]
            from_state = fadep * dot(b_low, g_low)
            dx = jnp.where(left, sides[0], sides[1]) + from_state
            dact[rows, lanes] = dtp * dx + skip[:, lanes] * dy
            grown = low(paired(grow, pair) * dy)
            dc = dc + dot_rows(grown, low(e))
            db = db + dot_rows(low(x * fadep), g_low)
            dt_part = dt_part + dot_full(v * dx, pick)
            out_part = out_part + dot_full(dy * ymix[rows, lanes], pick)
            ends = wholep * jnp.sum(e * g, axis=0, keepdims=True) + jnp.sum(
                x * from_state, axis=0, keepdims=True
            )
            end_part = end_part + dot_full(jnp.broadcast_to(ends, (8, LANES)), pick)
            leave[:, lanes] = g * wholep + dot(c_t, grown)
        d_in = dinner[...]
        dact[rows, INNER : INNER + STATE] = db + dot(low(d_in), c_low)
        dact[rows, INNER + STATE : CONV_CH] = dc + dot(low(d_in.T), b_low)
        dcum = out_part - dt * dt_part
        dcum = dcum + jnp.where(grid_of((SPAN, LANES), 0) == SPAN - 1, end_part[0:1], 0.0)
        rate = dot_full(triu, dcum)
        raw = ur[rows, CONV_CH:].astype(jnp.float32) + dtb[:, :HEADS]
        dr = (dt_part + a_neg[...] * rate)[:, :HEADS] * jax.nn.sigmoid(raw)
        gp[rows, CONV_CH:] = low(dr)
        dheads[0:1, :HEADS] += jnp.sum(dr, axis=0, keepdims=True)
        dheads[1:2] += jnp.sum(dt * rate, axis=0, keepdims=True) * a_neg[...]
        return carry

    lax.fori_loop(0, blocks, span, 0)
    upad[0:8] = rim[...].astype(jnp.float32)
    upad[8 : 8 + count] = ur[:, :CONV_CH].astype(jnp.float32)
    dcp[0:8] = jnp.zeros((8, CONV_CH), jnp.float32)
    dcp[8 + count : 16 + count] = jnp.zeros((8, CONV_CH), jnp.float32)
    dconv_w[...] = jnp.zeros_like(dconv_w)
    for first in range(0, CONV_CH, 256):
        columns = slice(first, first + 256)
        summed = conv_at(upad, conv_w, conv_b, count, columns)
        sig = jax.nn.sigmoid(summed)
        dconv = dact[:, columns] * (sig * (1.0 + summed * (1.0 - sig)))
        dcp[8 : 8 + count, columns] = dconv
        for k in range(CONV):
            dconv_w[k : k + 1, columns] = jnp.sum(
                dconv * upad[5 + k : 5 + k + count, columns], axis=0, keepdims=True
            )
        dconv_w[CONV : CONV + 1, columns] = jnp.sum(dconv, axis=0, keepdims=True)
        du = conv_w[0:1, columns] * dcp[3 : 3 + count + 8, columns]
        for k in range(1, CONV):
            du = du + conv_w[k : k + 1, columns] * dcp[3 - k : 3 - k + count + 8, columns]
        du_rim[:, columns] = du[0:8]
        du_tail[:, columns] = du[count : count + 8]
        gp[:, columns] = low(du[8:])


def local_call(kernel, outs, scratch, flops):
    return pl.pallas_call(
        kernel,
        out_shape=[jax.ShapeDtypeStruct(shape, kind) for shape, kind in outs],
        out_specs=[pl.BlockSpec(memory_space=pltpu.VMEM)] * len(outs),
        scratch_shapes=[pltpu.VMEM(shape, jnp.float32) for shape in scratch],
        compiler_params=pltpu.CompilerParams(vmem_limit_bytes=vmem_bytes),
        cost_estimate=pl.CostEstimate(flops=flops, bytes_accessed=20_000_000, transcendentals=0),
    )


def total_kernel(n, vec, square, total, squares, land, mine, sq_land, sq_mine, s1, r1, s2, r2, s3, r3):
    me = lax.axis_index("fsdp")
    rows = land.shape[1]
    barrier = pltpu.get_barrier_semaphore()

    def peer(k):
        return lax.rem(me + k, n)

    def greet(k, carry):
        pl.semaphore_signal(
            barrier, inc=1, device_id={"fsdp": peer(k)}, device_id_type=pl.DeviceIdType.MESH
        )
        return carry

    lax.fori_loop(1, n, greet, 0)
    pl.semaphore_wait(barrier, n - 1)

    def remote(k, src, dst, send, recv):
        return pltpu.make_async_remote_copy(
            src_ref=src,
            dst_ref=dst,
            send_sem=send.at[k],
            recv_sem=recv.at[k],
            device_id={"fsdp": peer(k)},
            device_id_type=pl.DeviceIdType.MESH,
        )

    def share(k):
        chunk = pl.ds(pl.multiple_of(peer(k) * rows, 8), rows)
        return remote(k, vec.at[chunk], land.at[k], s1, r1)

    def part(k):
        return remote(k, square, sq_land.at[k], s3, r3)

    def whole(k):
        chunk = pl.ds(pl.multiple_of(me * rows, 8), rows)
        return remote(k, mine, total.at[chunk], s2, r2)

    def each(act):
        def step(k, carry):
            act(k)
            return carry

        lax.fori_loop(1, n, step, 0)

    def begin(k):
        share(k).start()
        part(k).start()

    each(begin)
    own = pl.ds(pl.multiple_of(me * rows, 8), rows)
    each(lambda k: share(k).wait())
    summed = vec[own, :]
    for k in range(1, n):
        summed = summed + land[k]
    mine[...] = summed
    total[own, :] = summed
    each(lambda k: whole(k).start())
    each(lambda k: part(k).wait())
    gathered = square[...]
    for k in range(1, n):
        gathered = gathered + sq_land[k]
    squares[...] = gathered
    each(lambda k: whole(k).wait())


def total_call(n, vec, square):
    rows = vec.shape[0] // n
    dma = pltpu.SemaphoreType.DMA((n,))
    return pl.pallas_call(
        functools.partial(total_kernel, n),
        out_shape=[
            jax.ShapeDtypeStruct(vec.shape, jnp.float32),
            jax.ShapeDtypeStruct(square.shape, jnp.float32),
        ],
        in_specs=[pl.BlockSpec(memory_space=pltpu.VMEM)] * 2,
        out_specs=[pl.BlockSpec(memory_space=pltpu.VMEM)] * 2,
        scratch_shapes=[
            pltpu.VMEM((n, rows, LANES), jnp.float32),
            pltpu.VMEM((rows, LANES), jnp.float32),
            pltpu.VMEM((n, 8, LANES), jnp.float32),
            pltpu.VMEM((8, LANES), jnp.float32),
        ]
        + [dma] * 6,
        compiler_params=pltpu.CompilerParams(collective_id=0, has_side_effects=True),
    )(vec, square)


def adam_step(weight, grad, first, second, rate, decay):
    first_new = beta_one * first + (1.0 - beta_one) * grad
    second_new = beta_two * second + (1.0 - beta_two) * grad * grad
    first_hat = first_new / (1.0 - beta_one**STEP)
    second_hat = second_new / (1.0 - beta_two**STEP)
    weight_new = weight * (1.0 - rate * decay) - rate * first_hat / (
        jnp.sqrt(second_hat) + adam_eps
    )
    return (weight_new, first_new, second_new)


def passed_along(value, axis, steps):
    count = lax.axis_size(axis)
    first, last = (max(0, -steps), min(count, count - steps))
    return lax.ppermute(value, axis, [(source, source + steps) for source in range(first, last)])


def carried(value, decay, axis, steps):
    arrived = passed_along(low(value), axis, steps)
    for _ in range(lax.axis_size(axis) - 2):
        arrived = passed_along(low(value + decay * arrived.astype(jnp.float32)), axis, steps)
    return arrived


def summed_over(value, axis):
    if lax.axis_size(axis) == 2:
        return value.astype(jnp.float32) + lax.ppermute(value, axis, [(0, 1), (1, 0)]).astype(
            jnp.float32
        )
    return lax.psum(value.astype(jnp.float32), axis)


def head_lanes(values):
    return jnp.repeat(values, HEAD_DIM)[None]


def shards(
    tokens,
    cotangent,
    in_weight,
    out_weight,
    small_params,
    in_first,
    in_second,
    out_first,
    out_second,
    small_first,
    small_second,
):
    inputs = tokens[0].astype(jnp.float32)
    upstream_low = cotangent[0]
    upstream = upstream_low.astype(jnp.float32)
    count = inputs.shape[0]
    blocks = count // SPAN
    fsdp = lax.axis_size("fsdp")
    f32, bf16 = (jnp.float32, jnp.bfloat16)

    def gathered(shard):
        return lax.all_gather(low(shard), "fsdp", axis=0, tiled=True)

    win_ur = gathered(in_weight[:, INNER:])
    half = out_weight.shape[0] // 2
    rest = gathered(jnp.concatenate([in_weight[:, :INNER], out_weight[:half], out_weight[half:]], axis=1))
    win_z = rest[:, :INNER]
    wout = rest[:, INNER:].reshape(fsdp, half, 2, D).swapaxes(1, 2).reshape(INNER, D)

    cuts = [D, D + INNER, D + INNER + CONV * CONV_CH, D + INNER + (CONV + 1) * CONV_CH]
    gain_in = small_params[: cuts[0]]
    gain_y = small_params[cuts[0] : cuts[1]][None]
    conv_w = small_params[cuts[1] : cuts[2]].reshape(CONV, CONV_CH)
    conv_b = small_params[cuts[2] : cuts[3]][None]
    dt_bias, a_log, d_skip = small_params[cuts[3] :].reshape(3, HEADS)
    dtb = jnp.pad(dt_bias, (0, LANES - HEADS))[None]
    a_neg = jnp.pad(-jnp.exp(a_log), (0, LANES - HEADS))[None]
    skip = head_lanes(d_skip)

    normed_in, pull_norm = jax.vjp(rms_scale, inputs, gain_in)
    normed_low = low(normed_in)
    ur = dot(normed_low, win_ur).astype(bf16)
    rim = passed_along(ur[count - 8 :, :CONV_CH], "seq", 1)
    wide, heads = ((count, INNER), (count, LANES))
    act, step, cum, yraw, entering, dev_state = local_call(
        scan_kernel,
        [
            ((count, CONV_CH), f32),
            (heads, f32),
            (heads, f32),
            (wide, f32),
            ((blocks, STATE, INNER), f32),
            ((STATE, INNER), f32),
        ],
        [(count + 8, CONV_CH)],
        8_000_000_000,
    )(ur, rim, conv_w, conv_b, dtb, a_neg)
    dev_decay = head_lanes(jnp.exp(jnp.sum(cum[SPAN - 1 :: SPAN, :HEADS], axis=0)))
    start = carried(dev_state, dev_decay, "seq", 1)
    z = dot(normed_low, win_z).astype(bf16)
    grad_normed = dot_rows(upstream_low, wout)
    ymix, out_low, dz, dy, gate_sums, dstart = local_call(
        gate_kernel,
        [
            (wide, f32),
            (wide, bf16),
            (wide, bf16),
            (wide, f32),
            ((8, INNER), f32),
            ((STATE, INNER), f32),
        ],
        [(STATE, INNER), (8, INNER)],
        8_000_000_000,
    )(yraw, act, cum, start, z, grad_normed, gain_y, skip)
    later = carried(dstart, dev_decay, "seq", -1)

    def shared(grad):
        return lax.psum_scatter(low(grad), "fsdp", scatter_dimension=0, tiled=True)

    grad_z = low(dot(normed_low.T, dz)).reshape(fsdp, half, INNER)
    grad_wout = low(dot(out_low.T, upstream_low)).reshape(fsdp, 2 * half, D)
    own_rest = shared(
        jnp.concatenate([grad_z, grad_wout[:, :half], grad_wout[:, half:]], axis=2).reshape(
            fsdp * half, 2 * INNER
        )
    )
    output = low(inputs + dot(out_low, wout))[None]
    gp, du_tail, du_rim, dconv, dheads = local_call(
        back_kernel,
        [
            ((count, UR), bf16),
            ((8, CONV_CH), f32),
            ((8, CONV_CH), f32),
            ((8, CONV_CH), f32),
            ((8, LANES), f32),
        ],
        [
            (count + 8, CONV_CH),
            (count + 16, CONV_CH),
            (count, CONV_CH),
            (STATE, INNER),
            (blocks, STATE, INNER),
            (SPAN, SPAN),
        ],
        20_000_000_000,
    )(ur, rim, conv_w, conv_b, dtb, a_neg, act, step, cum, ymix, entering, start, later, dy, skip)
    rim_return = passed_along(du_rim, "seq", -1)
    gp = lax.dynamic_update_slice(gp, low(du_tail + rim_return), (count - 8, 0))
    own_ur = shared(dot(normed_low.T, gp))
    grad_normed_in = dot_rows(dz, win_z) + dot_rows(gp, win_ur)
    grad_inputs, grad_gain = pull_norm(grad_normed_in)
    input_grad = (upstream + grad_inputs)[None]
    grad_small = jnp.concatenate(
        [
            grad_gain,
            gate_sums[0],
            dconv[: CONV + 1].reshape(-1),
            dheads[0, :HEADS],
            dheads[1, :HEADS],
            jnp.sum(gate_sums[1].reshape(HEADS, HEAD_DIM), axis=1),
        ]
    )
    chunk = -(-SMALL // (fsdp * 8 * LANES)) * 8 * LANES
    grad_small = jnp.pad(grad_small, (0, chunk * fsdp - SMALL)).reshape(-1, LANES)
    grad_small = summed_over(grad_small, "seq")
    own_rest = summed_over(own_rest, "seq")
    own_ur = summed_over(own_ur, "seq")
    local_square = jnp.sum(own_rest * own_rest) + jnp.sum(own_ur * own_ur)
    grad_small, squares = total_call(fsdp, grad_small, jnp.full((8, LANES), local_square, f32))
    grad_small = grad_small.reshape(-1)[:SMALL]
    grad_norm = jnp.sqrt(squares[0, 0] + jnp.sum(grad_small * grad_small))
    factor = clip_level / jnp.maximum(grad_norm, clip_level)
    own_win = jnp.concatenate([own_rest[:, :INNER], own_ur], axis=1)
    own_wout = jnp.concatenate([own_rest[:, INNER : INNER + D], own_rest[:, INNER + D :]], axis=0)
    in_new, in_first_new, in_second_new = adam_step(
        in_weight, own_win * factor, in_first, in_second, rate_big, decay_big
    )
    out_new, out_first_new, out_second_new = adam_step(
        out_weight, own_wout * factor, out_first, out_second, rate_big, decay_big
    )
    small_new, small_first_new, small_second_new = adam_step(
        small_params, grad_small * factor, small_first, small_second, rate_small, 0.0
    )
    return (
        output,
        input_grad,
        in_new,
        in_first_new,
        in_second_new,
        out_new,
        out_first_new,
        out_second_new,
        small_new,
        small_first_new,
        small_second_new,
        grad_norm,
    )


def solution(mesh):
    return jax.shard_map(
        shards,
        mesh=mesh,
        in_specs=(
            P("fsdp", "seq", None),
            P("fsdp", "seq", None),
            P("fsdp", None),
            P("fsdp", None),
            P(),
            P("fsdp", None),
            P("fsdp", None),
            P("fsdp", None),
            P("fsdp", None),
            P(),
            P(),
        ),
        out_specs=(
            P("fsdp", "seq", None),
            P("fsdp", "seq", None),
            P("fsdp", None),
            P("fsdp", None),
            P("fsdp", None),
            P("fsdp", None),
            P("fsdp", None),
            P("fsdp", None),
            P(),
            P(),
            P(),
            P(),
        ),
        check_vma=False,
    )
```

```python
import jax
import jax.numpy as jnp
from jax import lax
from jax.experimental import pallas as pl
from jax.experimental.pallas import tpu as pltpu
import functools
from jax.sharding import PartitionSpec as P

D = 768
HEADS = 24
STATE = 128
HEAD_DIM = 64
CONV = 4
SPAN = 256
STEP = 10
INNER = 1536
CONV_CH = 1792
PROJ = 3352


norm_eps = 1e-05
beta_one = 0.9
beta_two = 0.999
rate_big = 0.05
rate_small = 0.2
decay_big = 0.1
clip_level = 1.0
adam_eps = 1e-08
far_below = -1e30
highest = lax.Precision.HIGHEST


UR = PROJ - INNER
URP = CONV_CH + 128
LANES = 128
PAIRS = INNER // LANES
SMALL = D + INNER + (CONV + 1) * CONV_CH + 3 * HEADS
vmem_bytes = 58 * 1024 * 1024


def rms_scale(values, gain):
    return values * lax.rsqrt(jnp.mean(values * values, axis=-1, keepdims=True) + norm_eps) * gain


def dot(a, b):
    return jnp.dot(a, b, preferred_element_type=jnp.float32)


def dot_rows(a, b):
    return lax.dot_general(a, b, (((1,), (1,)), ((), ())), preferred_element_type=jnp.float32)


def dot_full(a, b):
    return jnp.dot(a, b, precision=highest, preferred_element_type=jnp.float32)


def low(a):
    return a.astype(jnp.bfloat16)


def grid_of(shape, dim):
    return lax.broadcasted_iota(jnp.int32, shape, dim)


def expander():
    shape = (LANES, INNER)
    return (grid_of(shape, 1) // HEAD_DIM == grid_of(shape, 0)).astype(jnp.float32)


def pair_sum(pair):
    shape = (LANES, LANES)
    return (grid_of(shape, 0) // HEAD_DIM + 2 * pair == grid_of(shape, 1)).astype(jnp.float32)


def paired(values, pair):
    rows = values.shape[0]
    left = jnp.broadcast_to(values[:, 2 * pair : 2 * pair + 1], (rows, LANES))
    right = jnp.broadcast_to(values[:, 2 * pair + 1 : 2 * pair + 2], (rows, LANES))
    return jnp.where(grid_of((rows, LANES), 1) < HEAD_DIM, left, right)


def conv_at(upad, conv_w, conv_b, count, columns):
    summed = conv_b[:, columns] + conv_w[0:1, columns] * upad[5 : 5 + count, columns]
    for k in range(1, CONV):
        summed = summed + conv_w[k : k + 1, columns] * upad[5 + k : 5 + k + count, columns]
    return summed


def softplus(x):
    return jnp.maximum(x, 0.0) + jnp.log1p(jnp.exp(-jnp.abs(x)))


def span_rows(c):
    return pl.ds(pl.multiple_of(c * SPAN, SPAN), SPAN)


def scan_kernel(ur, rim, conv_w, conv_b, dtb, a_neg, act, step, cum_out, yraw, entering, state, upad):
    count = ur.shape[0]
    blocks = count // SPAN
    upad[0:8] = rim[...].astype(jnp.float32)
    upad[8 : 8 + count] = ur[:, :CONV_CH].astype(jnp.float32)
    for first in range(0, CONV_CH, 256):
        columns = slice(first, first + 256)
        summed = conv_at(upad, conv_w, conv_b, count, columns)
        act[:, columns] = summed * jax.nn.sigmoid(summed)
    step[...] = jnp.zeros_like(step)
    step[:, :HEADS] = softplus(ur[:, CONV_CH:UR].astype(jnp.float32) + dtb[:, :HEADS])
    state[...] = jnp.zeros_like(state)
    at, along = (grid_of((SPAN, SPAN), 0), grid_of((SPAN, SPAN), 1))
    causal = at >= along
    tril = causal.astype(jnp.float32)
    left = grid_of((SPAN, LANES), 1) < HEAD_DIM

    def span(c, carry):
        rows = span_rows(c)
        entering[pl.ds(c, 1)] = state[...][None]
        dt = step[rows, :]
        cum = dot_full(tril, dt * a_neg[...])
        cum_out[rows, :] = cum
        cum_t = cum.T
        last = cum[SPAN - 1 : SPAN, :]
        grow, tail, whole = (jnp.exp(cum), jnp.exp(last - cum) * dt, jnp.exp(last))
        b_vals = act[rows, INNER : INNER + STATE]
        b_t = low(b_vals.T)
        c_low = low(act[rows, INNER + STATE :])
        inner = dot_rows(c_low, low(b_vals))
        for pair in range(PAIRS):
            lanes = slice(pair * LANES, (pair + 1) * LANES)
            v = act[rows, lanes]
            x_low = low(v * paired(dt, pair))
            sides = []
            for h in (2 * pair, 2 * pair + 1):
                spread = jnp.where(causal, cum[:, h : h + 1] - cum_t[h : h + 1, :], far_below)
                sides.append(dot(low(jnp.exp(spread) * inner), x_low))
            was = state[:, lanes]
            yraw[rows, lanes] = jnp.where(left, sides[0], sides[1]) + paired(grow, pair) * dot(
                c_low, low(was)
            )
            state[:, lanes] = was * paired(whole, pair) + dot(b_t, low(v * paired(tail, pair)))
        return carry

    lax.fori_loop(0, blocks, span, 0)


def gate_kernel(yraw, act, cum_ref, start, z_ref, up, gain, skip, ymix, out, dz, dy, sums, dstart, held, run):
    count = yraw.shape[0]
    blocks = count // SPAN
    expand = expander()
    held[...] = start[...].astype(jnp.float32)
    run[...] = jnp.ones_like(run)
    sums[...] = jnp.zeros_like(sums)
    dstart[...] = jnp.zeros_like(dstart)

    def span(c, carry):
        rows = span_rows(c)
        cum = cum_ref[rows, :]
        grow = dot_full(jnp.exp(cum), expand)
        c_vals = act[rows, INNER + STATE : CONV_CH]
        raw = yraw[rows, :] + grow * dot(low(c_vals), low(held[...]))
        ymix[rows, :] = raw
        v = act[rows, :INNER]
        scanned = raw + skip[...] * v
        z = z_ref[rows, :].astype(jnp.float32)
        sig = jax.nn.sigmoid(z)
        gated = scanned * (z * sig)
        scale = lax.rsqrt(jnp.mean(gated * gated, axis=1, keepdims=True) + norm_eps)
        unit = gated * scale
        out[rows, :] = low(unit * gain[...])
        grad = up[rows, :]
        sums[0:1] += jnp.sum(grad * unit, axis=0, keepdims=True)
        grad = grad * gain[...]
        grad = scale * (grad - unit * jnp.mean(grad * unit, axis=1, keepdims=True))
        dz[rows, :] = low(grad * scanned * (sig * (1.0 + z * (1.0 - sig))))
        grad = grad * (z * sig)
        dy[rows, :] = grad
        sums[1:2] += jnp.sum(grad * v, axis=0, keepdims=True)
        dstart[...] += run[0:1] * dot(low(c_vals.T), low(grow * grad))
        whole = grow[SPAN - 1 : SPAN, :]
        held[...] = held[...] * whole
        run[...] = run[...] * whole
        return carry

    lax.fori_loop(0, blocks, span, 0)


def back_kernel(
    ur, rim, conv_w, conv_b, dtb, a_neg, act, step, cum_ref, ymix, entering, start, later, dy_ref, skip,
    gp, du_tail, du_rim, dconv_w, dheads, upad, dcp, dact, leave, before, dinner,
):
    count = ur.shape[0]
    blocks = count // SPAN
    dheads[...] = jnp.zeros_like(dheads)
    leave[...] = later[...].astype(jnp.float32)
    at, along = (grid_of((SPAN, SPAN), 0), grid_of((SPAN, SPAN), 1))
    causal = at <= along
    triu = causal.astype(jnp.float32)
    left = grid_of((SPAN, LANES), 1) < HEAD_DIM
    expand = expander()
    before[0] = start[...].astype(jnp.float32)
    for c in range(1, blocks):
        ends = jnp.exp(jnp.broadcast_to(cum_ref[c * SPAN - 1 : c * SPAN, :], (8, LANES)))
        before[c] = before[c - 1] * dot_full(ends, expand)[0:1]

    def span(lap, carry):
        c = blocks - 1 - lap
        rows = span_rows(c)
        dt, cum = (step[rows, :], cum_ref[rows, :])
        cum_t = cum.T
        last = cum[SPAN - 1 : SPAN, :]
        grow, fade, whole = (jnp.exp(cum), jnp.exp(last - cum), jnp.exp(last))
        b_vals, c_vals = (act[rows, INNER : INNER + STATE], act[rows, INNER + STATE : CONV_CH])
        b_low, c_low, c_t = (low(b_vals), low(c_vals), low(c_vals.T))
        inner = dot_rows(b_low, c_low)
        db = jnp.zeros((SPAN, STATE), jnp.float32)
        dc = jnp.zeros((SPAN, STATE), jnp.float32)
        dt_part = jnp.zeros((SPAN, LANES), jnp.float32)
        out_part = jnp.zeros((SPAN, LANES), jnp.float32)
        end_part = jnp.zeros((8, LANES), jnp.float32)
        dinner[...] = jnp.zeros_like(dinner)
        for pair in range(PAIRS):
            lanes = slice(pair * LANES, (pair + 1) * LANES)
            pick = pair_sum(pair)
            v, dy = (act[rows, lanes], dy_ref[rows, lanes])
            dtp, fadep, wholep = (paired(dt, pair), paired(fade, pair), paired(whole, pair))
            x = v * dtp
            dy_low = low(dy)
            sides = []
            for h, mine in ((2 * pair, left), (2 * pair + 1, ~left)):
                decay = jnp.exp(
                    jnp.where(causal, cum_t[h : h + 1, :] - cum[:, h : h + 1], far_below)
                )
                sides.append(dot(low(decay * inner), dy_low))
                dinner[...] += decay * dot_rows(low(jnp.where(mine, x, 0.0)), dy_low)
            g = leave[:, lanes]
            g_low = low(g)
            e = entering[pl.ds(c, 1), :, lanes][0] + before[pl.ds(c, 1), :, lanes][0]
            from_state = fadep * dot(b_low, g_low)
            dx = jnp.where(left, sides[0], sides[1]) + from_state
            dact[rows, lanes] = dtp * dx + skip[:, lanes] * dy
            grown = low(paired(grow, pair) * dy)
            dc = dc + dot_rows(grown, low(e))
            db = db + dot_rows(low(x * fadep), g_low)
            dt_part = dt_part + dot_full(v * dx, pick)
            out_part = out_part + dot_full(dy * ymix[rows, lanes], pick)
            ends = wholep * jnp.sum(e * g, axis=0, keepdims=True) + jnp.sum(
                x * from_state, axis=0, keepdims=True
            )
            end_part = end_part + dot_full(jnp.broadcast_to(ends, (8, LANES)), pick)
            leave[:, lanes] = g * wholep + dot(c_t, grown)
        d_in = dinner[...]
        dact[rows, INNER : INNER + STATE] = db + dot(low(d_in), c_low)
        dact[rows, INNER + STATE : CONV_CH] = dc + dot(low(d_in.T), b_low)
        dcum = out_part - dt * dt_part
        dcum = dcum + jnp.where(grid_of((SPAN, LANES), 0) == SPAN - 1, end_part[0:1], 0.0)
        rate = dot_full(triu, dcum)
        raw = ur[rows, CONV_CH:UR].astype(jnp.float32) + dtb[:, :HEADS]
        dr = (dt_part + a_neg[...] * rate)[:, :HEADS] * jax.nn.sigmoid(raw)
        gp[rows, CONV_CH:] = jnp.zeros((SPAN, URP - CONV_CH), jnp.bfloat16)
        gp[rows, CONV_CH:UR] = low(dr)
        dheads[0:1, :HEADS] += jnp.sum(dr, axis=0, keepdims=True)
        dheads[1:2] += jnp.sum(dt * rate, axis=0, keepdims=True) * a_neg[...]
        return carry

    lax.fori_loop(0, blocks, span, 0)
    upad[0:8] = rim[...].astype(jnp.float32)
    upad[8 : 8 + count] = ur[:, :CONV_CH].astype(jnp.float32)
    dcp[0:8] = jnp.zeros((8, CONV_CH), jnp.float32)
    dcp[8 + count : 16 + count] = jnp.zeros((8, CONV_CH), jnp.float32)
    dconv_w[...] = jnp.zeros_like(dconv_w)
    for first in range(0, CONV_CH, 256):
        columns = slice(first, first + 256)
        summed = conv_at(upad, conv_w, conv_b, count, columns)
        sig = jax.nn.sigmoid(summed)
        dconv = dact[:, columns] * (sig * (1.0 + summed * (1.0 - sig)))
        dcp[8 : 8 + count, columns] = dconv
        for k in range(CONV):
            dconv_w[k : k + 1, columns] = jnp.sum(
                dconv * upad[5 + k : 5 + k + count, columns], axis=0, keepdims=True
            )
        dconv_w[CONV : CONV + 1, columns] = jnp.sum(dconv, axis=0, keepdims=True)
        du = conv_w[0:1, columns] * dcp[3 : 3 + count + 8, columns]
        for k in range(1, CONV):
            du = du + conv_w[k : k + 1, columns] * dcp[3 - k : 3 - k + count + 8, columns]
        du_rim[:, columns] = du[0:8]
        du_tail[:, columns] = du[count : count + 8]
        gp[:, columns] = low(du[8:])


def local_call(kernel, outs, scratch, flops):
    return pl.pallas_call(
        kernel,
        out_shape=[jax.ShapeDtypeStruct(shape, kind) for shape, kind in outs],
        out_specs=[pl.BlockSpec(memory_space=pltpu.VMEM)] * len(outs),
        scratch_shapes=[pltpu.VMEM(shape, jnp.float32) for shape in scratch],
        compiler_params=pltpu.CompilerParams(vmem_limit_bytes=vmem_bytes),
        cost_estimate=pl.CostEstimate(flops=flops, bytes_accessed=20_000_000, transcendentals=0),
    )


def total_kernel(n, vec, square, total, squares, land, mine, sq_land, sq_mine, s1, r1, s2, r2, s3, r3):
    me = lax.axis_index("fsdp")
    rows = land.shape[1]
    barrier = pltpu.get_barrier_semaphore()

    def peer(k):
        return lax.rem(me + k, n)

    def greet(k, carry):
        pl.semaphore_signal(
            barrier, inc=1, device_id={"fsdp": peer(k)}, device_id_type=pl.DeviceIdType.MESH
        )
        return carry

    lax.fori_loop(1, n, greet, 0)
    pl.semaphore_wait(barrier, n - 1)

    def remote(k, src, dst, send, recv):
        return pltpu.make_async_remote_copy(
            src_ref=src,
            dst_ref=dst,
            send_sem=send.at[k],
            recv_sem=recv.at[k],
            device_id={"fsdp": peer(k)},
            device_id_type=pl.DeviceIdType.MESH,
        )

    def share(k):
        chunk = pl.ds(pl.multiple_of(peer(k) * rows, 8), rows)
        return remote(k, vec.at[chunk], land.at[k], s1, r1)

    def part(k):
        return remote(k, square, sq_land.at[k], s3, r3)

    def whole(k):
        chunk = pl.ds(pl.multiple_of(me * rows, 8), rows)
        return remote(k, mine, total.at[chunk], s2, r2)

    def each(act):
        def step(k, carry):
            act(k)
            return carry

        lax.fori_loop(1, n, step, 0)

    def begin(k):
        share(k).start()
        part(k).start()

    each(begin)
    own = pl.ds(pl.multiple_of(me * rows, 8), rows)
    each(lambda k: share(k).wait())
    summed = vec[own, :]
    for k in range(1, n):
        summed = summed + land[k]
    mine[...] = summed
    total[own, :] = summed
    each(lambda k: whole(k).start())
    each(lambda k: part(k).wait())
    gathered = square[...]
    for k in range(1, n):
        gathered = gathered + sq_land[k]
    squares[...] = gathered
    each(lambda k: whole(k).wait())


def total_call(n, vec, square):
    rows = vec.shape[0] // n
    dma = pltpu.SemaphoreType.DMA((n,))
    return pl.pallas_call(
        functools.partial(total_kernel, n),
        out_shape=[
            jax.ShapeDtypeStruct(vec.shape, jnp.float32),
            jax.ShapeDtypeStruct(square.shape, jnp.float32),
        ],
        in_specs=[pl.BlockSpec(memory_space=pltpu.VMEM)] * 2,
        out_specs=[pl.BlockSpec(memory_space=pltpu.VMEM)] * 2,
        scratch_shapes=[
            pltpu.VMEM((n, rows, LANES), jnp.float32),
            pltpu.VMEM((rows, LANES), jnp.float32),
            pltpu.VMEM((n, 8, LANES), jnp.float32),
            pltpu.VMEM((8, LANES), jnp.float32),
        ]
        + [dma] * 6,
        compiler_params=pltpu.CompilerParams(collective_id=0, has_side_effects=True),
    )(vec, square)


def places(n):
    me = lax.axis_index("fsdp")
    chip, core = (me // 2, lax.rem(me, 2))
    chips = n // 2

    def ahead(k):
        return 2 * lax.rem(chip + k, chips) + core

    def behind(k):
        return 2 * lax.rem(chip - k + chips, chips) + core

    return (me, me + 1 - 2 * core, core, chips, ahead, behind)


def greeted(peers, sibling, count):
    barrier = pltpu.get_barrier_semaphore()
    mesh_ids = pl.DeviceIdType.MESH
    pl.semaphore_signal(barrier, inc=1, device_id={"fsdp": sibling}, device_id_type=mesh_ids)

    def greet(k, carry):
        pl.semaphore_signal(barrier, inc=1, device_id={"fsdp": peers(k)}, device_id_type=mesh_ids)
        return carry

    lax.fori_loop(1, count, greet, 0)
    pl.semaphore_wait(barrier, count)


def copy_to(place, k, src, dst, send, recv):
    return pltpu.make_async_remote_copy(
        src_ref=src,
        dst_ref=dst,
        send_sem=send.at[k],
        recv_sem=recv.at[k],
        device_id={"fsdp": place},
        device_id_type=pl.DeviceIdType.MESH,
    )


def loop(first, end, act):
    def step(k, carry):
        act(k)
        return carry

    lax.fori_loop(first, end, step, 0)


def gather_kernel(n, shard, whole, s1, r1, s2, r2):
    me, sibling, core, chips, ahead, behind = places(n)
    greeted(ahead, sibling, chips)

    def across(k):
        return copy_to(ahead(k), k, shard, whole.at[me], s1, r1)

    def beside(k):
        block = whole.at[behind(k)]
        return copy_to(sibling, k, block, block, s2, r2)

    first = copy_to(sibling, 0, shard, whole.at[me], s2, r2)
    loop(1, chips, lambda k: across(k).start())
    first.start()
    whole[pl.ds(me, 1)] = shard[...][None]

    def hand_on(k):
        across(k).wait_recv()
        beside(k).start()

    loop(1, chips, hand_on)
    first.wait()
    loop(1, chips, lambda k: beside(k).wait())
    loop(1, chips, lambda k: across(k).wait_send())


def gather_call(n, shard):
    dma = pltpu.SemaphoreType.DMA((n // 2,))
    return pl.pallas_call(
        functools.partial(gather_kernel, n),
        out_shape=jax.ShapeDtypeStruct((n,) + shard.shape, shard.dtype),
        in_specs=[pl.BlockSpec(memory_space=pltpu.VMEM)],
        out_specs=pl.BlockSpec(memory_space=pltpu.VMEM),
        scratch_shapes=[dma] * 4,
        compiler_params=pltpu.CompilerParams(
            collective_id=1, has_side_effects=True, vmem_limit_bytes=vmem_bytes
        ),
    )(shard)


def scatter_kernel(n, grads, total, near, pre, far, s1, r1, s2, r2):
    me, sibling, core, chips, ahead, behind = places(n)
    greeted(ahead, sibling, chips)

    def beside(k):
        theirs = ahead(k) + 1 - 2 * core
        return copy_to(sibling, k, grads.at[theirs], near.at[k], s1, r1)

    def across(k):
        return copy_to(ahead(k), k, pre.at[k], far.at[k], s2, r2)

    def both(k):
        beside(k).wait_recv()
        return grads[pl.ds(ahead(k), 1)].astype(jnp.float32) + near[pl.ds(k, 1)].astype(jnp.float32)

    loop(1, chips, lambda k: beside(k).start())
    beside(0).start()

    def pass_on(k):
        pre[pl.ds(k, 1)] = low(both(k))
        across(k).start()

    loop(1, chips, pass_on)
    total[...] = both(0)[0]

    def add(k):
        across(k).wait_recv()
        total[...] += far[pl.ds(k, 1)].astype(jnp.float32)[0]

    loop(1, chips, add)
    loop(0, chips, lambda k: beside(k).wait_send())
    loop(1, chips, lambda k: across(k).wait_send())


def scatter_call(n, grads):
    dma = pltpu.SemaphoreType.DMA((n // 2,))
    block = grads.shape[1:]
    return pl.pallas_call(
        functools.partial(scatter_kernel, n),
        out_shape=jax.ShapeDtypeStruct(block, jnp.float32),
        in_specs=[pl.BlockSpec(memory_space=pltpu.VMEM)],
        out_specs=pl.BlockSpec(memory_space=pltpu.VMEM),
        scratch_shapes=[pltpu.VMEM((n // 2,) + block, grads.dtype)] * 3 + [dma] * 4,
        compiler_params=pltpu.CompilerParams(
            collective_id=2, has_side_effects=True, vmem_limit_bytes=vmem_bytes
        ),
    )(grads)


def adam_step(weight, grad, first, second, rate, decay):
    first_new = beta_one * first + (1.0 - beta_one) * grad
    second_new = beta_two * second + (1.0 - beta_two) * grad * grad
    first_hat = first_new / (1.0 - beta_one**STEP)
    second_hat = second_new / (1.0 - beta_two**STEP)
    weight_new = weight * (1.0 - rate * decay) - rate * first_hat / (
        jnp.sqrt(second_hat) + adam_eps
    )
    return (weight_new, first_new, second_new)


def passed_along(value, axis, steps):
    count = lax.axis_size(axis)
    first, last = (max(0, -steps), min(count, count - steps))
    return lax.ppermute(value, axis, [(source, source + steps) for source in range(first, last)])


def carried(value, decay, axis, steps):
    arrived = passed_along(low(value), axis, steps)
    for _ in range(lax.axis_size(axis) - 2):
        arrived = passed_along(low(value + decay * arrived.astype(jnp.float32)), axis, steps)
    return arrived


def summed_over(value, axis):
    if lax.axis_size(axis) == 2:
        return value.astype(jnp.float32) + lax.ppermute(value, axis, [(0, 1), (1, 0)]).astype(
            jnp.float32
        )
    return lax.psum(value.astype(jnp.float32), axis)


def head_lanes(values):
    return jnp.repeat(values, HEAD_DIM)[None]


def shards(
    tokens,
    cotangent,
    in_weight,
    out_weight,
    small_params,
    in_first,
    in_second,
    out_first,
    out_second,
    small_first,
    small_second,
):
    inputs = tokens[0].astype(jnp.float32)
    upstream_low = cotangent[0]
    upstream = upstream_low.astype(jnp.float32)
    count = inputs.shape[0]
    blocks = count // SPAN
    fsdp = lax.axis_size("fsdp")
    f32, bf16 = (jnp.float32, jnp.bfloat16)

    def gathered(shard):
        return lax.all_gather(low(shard), "fsdp", axis=0, tiled=True)

    win_ur = gather_call(fsdp, jnp.pad(low(in_weight[:, INNER:]), ((0, 0), (0, URP - UR))))
    win_ur = win_ur.reshape(D, URP)
    half = out_weight.shape[0] // 2
    rest = gathered(jnp.concatenate([in_weight[:, :INNER], out_weight[:half], out_weight[half:]], axis=1))
    win_z = rest[:, :INNER]
    wout = rest[:, INNER:].reshape(fsdp, half, 2, D).swapaxes(1, 2).reshape(INNER, D)

    cuts = [D, D + INNER, D + INNER + CONV * CONV_CH, D + INNER + (CONV + 1) * CONV_CH]
    gain_in = small_params[: cuts[0]]
    gain_y = small_params[cuts[0] : cuts[1]][None]
    conv_w = small_params[cuts[1] : cuts[2]].reshape(CONV, CONV_CH)
    conv_b = small_params[cuts[2] : cuts[3]][None]
    dt_bias, a_log, d_skip = small_params[cuts[3] :].reshape(3, HEADS)
    dtb = jnp.pad(dt_bias, (0, LANES - HEADS))[None]
    a_neg = jnp.pad(-jnp.exp(a_log), (0, LANES - HEADS))[None]
    skip = head_lanes(d_skip)

    normed_in, pull_norm = jax.vjp(rms_scale, inputs, gain_in)
    normed_low = low(normed_in)
    ur = dot(normed_low, win_ur).astype(bf16)
    rim = passed_along(ur[count - 8 :, :CONV_CH], "seq", 1)
    wide, heads = ((count, INNER), (count, LANES))
    act, step, cum, yraw, entering, dev_state = local_call(
        scan_kernel,
        [
            ((count, CONV_CH), f32),
            (heads, f32),
            (heads, f32),
            (wide, f32),
            ((blocks, STATE, INNER), f32),
            ((STATE, INNER), f32),
        ],
        [(count + 8, CONV_CH)],
        8_000_000_000,
    )(ur, rim, conv_w, conv_b, dtb, a_neg)
    dev_decay = head_lanes(jnp.exp(jnp.sum(cum[SPAN - 1 :: SPAN, :HEADS], axis=0)))
    start = carried(dev_state, dev_decay, "seq", 1)
    z = dot(normed_low, win_z).astype(bf16)
    grad_normed = dot_rows(upstream_low, wout)
    ymix, out_low, dz, dy, gate_sums, dstart = local_call(
        gate_kernel,
        [
            (wide, f32),
            (wide, bf16),
            (wide, bf16),
            (wide, f32),
            ((8, INNER), f32),
            ((STATE, INNER), f32),
        ],
        [(STATE, INNER), (8, INNER)],
        8_000_000_000,
    )(yraw, act, cum, start, z, grad_normed, gain_y, skip)
    later = carried(dstart, dev_decay, "seq", -1)

    def shared(grad):
        return lax.psum_scatter(low(grad), "fsdp", scatter_dimension=0, tiled=True)

    grad_z = low(dot(normed_low.T, dz)).reshape(fsdp, half, INNER)
    grad_wout = low(dot(out_low.T, upstream_low)).reshape(fsdp, 2 * half, D)
    grad_rest = jnp.concatenate([grad_z, grad_wout[:, :half], grad_wout[:, half:]], axis=2)
    grad_rest, later = lax.optimization_barrier((grad_rest, later))
    own_rest = shared(grad_rest.reshape(fsdp * half, 2 * INNER))
    output = low(inputs + dot(out_low, wout))[None]
    gp, du_tail, du_rim, dconv, dheads = local_call(
        back_kernel,
        [
            ((count, URP), bf16),
            ((8, CONV_CH), f32),
            ((8, CONV_CH), f32),
            ((8, CONV_CH), f32),
            ((8, LANES), f32),
        ],
        [
            (count + 8, CONV_CH),
            (count + 16, CONV_CH),
            (count, CONV_CH),
            (STATE, INNER),
            (blocks, STATE, INNER),
            (SPAN, SPAN),
        ],
        20_000_000_000,
    )(ur, rim, conv_w, conv_b, dtb, a_neg, act, step, cum, ymix, entering, start, later, dy, skip)
    rim_return = passed_along(du_rim, "seq", -1)
    gp = lax.dynamic_update_slice(gp, low(du_tail + rim_return), (count - 8, 0))
    own_ur = scatter_call(fsdp, low(dot(normed_low.T, gp)).reshape(fsdp, half, URP))
    grad_normed_in = dot_rows(dz, win_z) + dot_rows(gp, win_ur)
    grad_inputs, grad_gain = pull_norm(grad_normed_in)
    input_grad = (upstream + grad_inputs)[None]
    grad_small = jnp.concatenate(
        [
            grad_gain,
            gate_sums[0],
            dconv[: CONV + 1].reshape(-1),
            dheads[0, :HEADS],
            dheads[1, :HEADS],
            jnp.sum(gate_sums[1].reshape(HEADS, HEAD_DIM), axis=1),
        ]
    )
    chunk = -(-SMALL // (fsdp * 8 * LANES)) * 8 * LANES
    grad_small = jnp.pad(grad_small, (0, chunk * fsdp - SMALL)).reshape(-1, LANES)
    grad_small = summed_over(grad_small, "seq")
    own_rest = summed_over(own_rest, "seq")
    own_ur = summed_over(low(own_ur), "seq")[:, :UR]
    local_square = jnp.sum(own_rest * own_rest) + jnp.sum(own_ur * own_ur)
    grad_small, squares = total_call(fsdp, grad_small, jnp.full((8, LANES), local_square, f32))
    grad_small = grad_small.reshape(-1)[:SMALL]
    grad_norm = jnp.sqrt(squares[0, 0] + jnp.sum(grad_small * grad_small))
    factor = clip_level / jnp.maximum(grad_norm, clip_level)
    own_win = jnp.concatenate([own_rest[:, :INNER], own_ur], axis=1)
    own_wout = jnp.concatenate([own_rest[:, INNER : INNER + D], own_rest[:, INNER + D :]], axis=0)
    in_new, in_first_new, in_second_new = adam_step(
        in_weight, own_win * factor, in_first, in_second, rate_big, decay_big
    )
    out_new, out_first_new, out_second_new = adam_step(
        out_weight, own_wout * factor, out_first, out_second, rate_big, decay_big
    )
    small_new, small_first_new, small_second_new = adam_step(
        small_params, grad_small * factor, small_first, small_second, rate_small, 0.0
    )
    return (
        output,
        input_grad,
        in_new,
        in_first_new,
        in_second_new,
        out_new,
        out_first_new,
        out_second_new,
        small_new,
        small_first_new,
        small_second_new,
        grad_norm,
    )


def solution(mesh):
    return jax.shard_map(
        shards,
        mesh=mesh,
        in_specs=(
            P("fsdp", "seq", None),
            P("fsdp", "seq", None),
            P("fsdp", None),
            P("fsdp", None),
            P(),
            P("fsdp", None),
            P("fsdp", None),
            P("fsdp", None),
            P("fsdp", None),
            P(),
            P(),
        ),
        out_specs=(
            P("fsdp", "seq", None),
            P("fsdp", "seq", None),
            P("fsdp", None),
            P("fsdp", None),
            P("fsdp", None),
            P("fsdp", None),
            P("fsdp", None),
            P("fsdp", None),
            P(),
            P(),
            P(),
            P(),
        ),
        check_vma=False,
    )
```
